1024 devices in a mesh: section: 8 (over y_lo, core), expert: 64 (over z, x), dp: 2 (over y_hi).
Axes of the slice: x: 8, y: 8 (y_hi: 2, y_lo: 4; y = y_hi * 4 + y_lo), z: 8, core: 2. Of those that a mesh axis runs over, the one named last changes fastest.
Arguments:
- carry: bfloat16 [16, 2, 4096, 1440], P('section', 'dp', 'expert'), may hold values from -6 to 6
- hidden_fwd: bfloat16 [8, 2, 64, 320, 1440], P('section', 'dp', 'expert'), may hold values from -6 to 6
- expert_weight: bfloat16 [8, 64, 1440, 1440], P('section', 'expert'), may hold values from -0.15625 to 0.15625
- expert_bias: bfloat16 [8, 64, 1440], P('section', 'expert'), may hold values from -3 to 3
- ids_fwd: int32 [8, 2, 4096, 4], P('section', 'dp', 'expert'), may hold values from 0 to 63, all different within a row; in each aligned block of 64 rows (0 to 63, 64 to 127, ..., all dimensions but the last counted through in order) at most 5 rows name the same one
- gates_fwd: float32 [8, 2, 4096, 4], P('section', 'dp', 'expert'), may hold values from 0.05 to 1
- ids_bwd: int32 [8, 2, 4096, 4], P('section', 'dp', 'expert'), may hold values from 0 to 63, all different within a row; in each aligned block of 64 rows (0 to 63, 64 to 127, ..., all dimensions but the last counted through in order) at most 5 rows name the same one
- gates_bwd: float32 [8, 2, 4096, 4], P('section', 'dp', 'expert'), may hold values from 0.05 to 1
Outputs:
- section_out: bfloat16 [8, 2, 4096, 1440], P('section', 'dp', 'expert')
- bias_grad: float32 [8, 64, 1440], P('section', 'expert', 'dp')
The draws below stay inside these ranges and needn't reach their ends.
Inputs may be any that keep to these rules, and one draw needn't show every extreme that they name: `ids_fwd`: each row names 4 different experts. Among the 64 rows of one device no expert is named more than 5 times, and in every draw some device names some expert exactly 5 times. `ids_bwd`: as for ids_fwd.
All inputs are finite; a program needn't handle non-finite values.
Results may differ from the reference program's by a relative error of at most 0.0085.
Values may be sent and summed in bfloat16 or wider, within the bound.
A program may use at most 32 MiB of HBM per device.

```python
import math
import jax
import jax.numpy as jnp
import numpy as np
from jax import lax

DW = 1440
FFW = 1440
TOP = 4
TOK_DEV = 64
EXPERTS = 64
CAP = 5
SLOTS = 320
TOKENS = 4096
SECTIONS = 8
REPLICAS = 2
N_EXPERT = 64


def level_of(rng, shape, split, smallest, largest):
    def one(dim, blocks):
        steps = jax.random.uniform(jax.random.fold_in(jax.random.fold_in(rng, 6), dim), (blocks,), jnp.float32, smallest / len(split), largest / len(split))
        return jnp.repeat(jnp.exp(steps), shape[dim] // blocks).reshape((-1,) + (1,) * (len(shape) - dim - 1))

    level = one(*split[0])
    for cut in split[1:]:
        level = level * one(*cut)
    return level


def assign_block(stream_key, own, number, rows, number_of, top, bound, slope):
    ranking = jax.random.permutation(stream_key, number_of)
    heavy_load, common = portions_of(number_of, rows * top, bound, slope, True), portions_of(number_of, rows * top, bound, slope, False)
    places = jnp.arange(number_of)

    def named(lengths, rotation):
        used = int((lengths > 0).sum())
        fixed = max(1, used // 4)
        passed = fixed + (places - fixed + rotation * (used - fixed)) % max(1, number_of - fixed)
        return jnp.zeros((number_of,), jnp.int32).at[ranking[jnp.where(places < fixed, places, passed)]].set(jnp.asarray(lengths, jnp.int32))

    lengths = jnp.where(number % 4 == 0, named(heavy_load, number // 4), named(common, number - number // 4 - 1))
    mixed = jax.random.permutation(jax.random.fold_in(own, 3), number_of)
    giver, taker = mixed[0:number_of // 2 * 2:2], mixed[1:number_of // 2 * 2:2]
    margin = jnp.minimum(lengths[giver] - 1, bound - lengths[taker]) // 2
    margin = jnp.where((giver == ranking[0]) | (taker == ranking[0]) | (lengths[taker] == 0), 0, jnp.maximum(margin, 0))
    passed = jax.random.randint(jax.random.fold_in(own, 4), (number_of // 2,), 0, 1 << 20) % (margin + 1)
    lengths = lengths.at[giver].add(-passed).at[taker].add(passed)
    members = jnp.searchsorted(jnp.cumsum(lengths), jnp.arange(rows * top), side="right").astype(jnp.int32)
    table = members.reshape(top, rows).T
    table = table[jax.random.permutation(jax.random.fold_in(own, 1), rows)]
    rotation = jax.random.randint(jax.random.fold_in(own, 2), (rows, 1), 0, top)
    return jnp.take_along_axis(table, (jnp.arange(top)[None, :] + rotation) % top, axis=1)


def portions_of(count, total, bound, slope, full):
    portions = [(1 << 20) // math.isqrt(rank ** slope) + 1 for rank in range(1, count + 1)]
    largest = bound if full else min(bound, max(-(-total // count), total * portions[0] // sum(portions)))
    least = 1 if total - largest >= count - 1 else 0
    given, spare = [largest] + [least] * (count - 1), total - largest - least * (count - 1)
    while spare > 0:
        free = [i for i in range(1, count) if given[i] < largest] or [i for i in range(1, count) if given[i] < bound]
        whole, remaining = sum([portions[i] for i in free]), spare
        for i in free:
            more = min(bound - given[i], max(1, remaining * portions[i] // whole), spare)
            given[i] = given[i] + more
            spare = spare - more
    return np.array(given)


def gaussian(key, shape, scale, bound, cuts=(), held_as=jnp.bfloat16):
    loudness = level_of(key, shape, cuts, -0.22, 0.18) if cuts else 1.0
    drawn = jax.random.normal(key, shape, jnp.float32) * scale * loudness
    return jnp.minimum(jnp.maximum(drawn, -bound), bound).astype(held_as)


def setup_inputs(seed: int = 0) -> dict:
    arg_keys = jax.random.split(jax.random.key(seed), 9)
    carry = gaussian(arg_keys[0], (2 * SECTIONS, REPLICAS, TOKENS, DW), 1.0, 6.0, ((0, 8), (1, 2), (2, 64)))
    hidden_fwd = gaussian(arg_keys[1], (SECTIONS, REPLICAS, EXPERTS, SLOTS, FFW), 1.0, 6.0, ((0, 8), (1, 2), (2, 64)))
    expert_weight = gaussian(arg_keys[2], (SECTIONS, EXPERTS, FFW, DW), FFW ** -0.5, 0.15625, ((0, 8), (1, 64)))
    expert_bias = gaussian(arg_keys[3], (SECTIONS, EXPERTS, DW), 0.5, 3.0, ((0, 8), (1, 64)))
    ids_fwd_keys = jax.random.split(jax.random.fold_in(arg_keys[4], 1), SECTIONS * REPLICAS * TOKENS // TOK_DEV)
    ids_fwd_turns = jax.random.permutation(jax.random.fold_in(arg_keys[4], 3), SECTIONS * REPLICAS * TOKENS // TOK_DEV)
    ids_fwd = jax.vmap(lambda own, number: assign_block(jax.random.fold_in(arg_keys[4], 2), own, number, TOK_DEV, EXPERTS, TOP, CAP, 2))(ids_fwd_keys, ids_fwd_turns).reshape((SECTIONS, REPLICAS, TOKENS, TOP))
    gates_fwd = jnp.clip(jnp.exp(math.log(1.0) - 2.9957323 * jax.random.uniform(arg_keys[5], (SECTIONS, REPLICAS, TOKENS, TOP), jnp.float32) ** level_of(arg_keys[5], (SECTIONS, REPLICAS, TOKENS, TOP), ((0, 8), (1, 2), (2, 64)), -0.2, 0.2)), 0.05, 1.0)
    ids_bwd_keys = jax.random.split(jax.random.fold_in(arg_keys[6], 1), SECTIONS * REPLICAS * TOKENS // TOK_DEV)
    ids_bwd_turns = jax.random.permutation(jax.random.fold_in(arg_keys[6], 3), SECTIONS * REPLICAS * TOKENS // TOK_DEV)
    ids_bwd = jax.vmap(lambda own, number: assign_block(jax.random.fold_in(arg_keys[6], 2), own, number, TOK_DEV, EXPERTS, TOP, CAP, 2))(ids_bwd_keys, ids_bwd_turns).reshape((SECTIONS, REPLICAS, TOKENS, TOP))
    gates_bwd = jnp.clip(jnp.exp(math.log(1.0) - 2.9957323 * jax.random.uniform(arg_keys[7], (SECTIONS, REPLICAS, TOKENS, TOP), jnp.float32) ** level_of(arg_keys[7], (SECTIONS, REPLICAS, TOKENS, TOP), ((0, 8), (1, 2), (2, 64)), -0.2, 0.2)), 0.05, 1.0)
    return dict(carry=carry, hidden_fwd=hidden_fwd, expert_weight=expert_weight, expert_bias=expert_bias, ids_fwd=ids_fwd, gates_fwd=gates_fwd, ids_bwd=ids_bwd, gates_bwd=gates_bwd)


def ranks(ids):
    blocks = ids.reshape(SECTIONS, REPLICAS, N_EXPERT, TOK_DEV * TOP)
    onehot = (blocks[..., None] == jnp.arange(EXPERTS, dtype=jnp.int32)).astype(jnp.int32)
    before = jnp.cumsum(onehot, axis=3, dtype=jnp.int32) - onehot
    return jnp.sum(before * onehot, axis=4, dtype=jnp.int32)


def row_numbers(ids):
    slot_rank = ranks(ids)
    blocks = ids.reshape(SECTIONS, REPLICAS, N_EXPERT, TOK_DEV * TOP)
    offsets = (jnp.arange(N_EXPERT, dtype=jnp.int32) * CAP)[None, None, :, None]
    rows = blocks * SLOTS + offsets + slot_rank
    return rows.reshape(SECTIONS, REPLICAS, TOKENS * TOP).astype(jnp.int32)


def reference(carry, hidden_fwd, expert_weight, expert_bias, ids_fwd, gates_fwd, ids_bwd, gates_bwd):
    section_ids = jnp.arange(SECTIONS, dtype=jnp.int32)
    incoming = carry[2 * ((section_ids - 1) % SECTIONS) + 1]
    upstream = carry[2 * ((section_ids + 1) % SECTIONS)]
    row_index = row_numbers(ids_fwd)

    def forward_section(inputs):
        hidden, weight, bias, rows, residual, gates = inputs
        produced = jnp.einsum("resf,efd->resd", hidden.astype(jnp.float32), weight.astype(jnp.float32))
        produced = (produced + bias.astype(jnp.float32)[None, :, None, :]).astype(jnp.bfloat16)
        produced = produced.reshape(REPLICAS, EXPERTS * SLOTS, DW)
        picked = jnp.take_along_axis(produced, rows[:, :, None], axis=1)
        picked = picked.reshape(REPLICAS, TOKENS, TOP, DW).astype(jnp.float32)
        mixture = residual.astype(jnp.float32) + jnp.sum(gates[..., None] * picked, axis=2)
        return mixture.astype(jnp.bfloat16)

    section_out = lax.map(forward_section, (hidden_fwd, expert_weight, expert_bias, row_index, incoming, gates_fwd))

    def backward_section(inputs):
        gradient, gates, ids = inputs
        scaled = (gates[..., None] * gradient[:, :, None, :].astype(jnp.float32)).astype(jnp.bfloat16)
        scaled = scaled.reshape(REPLICAS, TOKENS * TOP, DW).astype(jnp.float32)
        onehot = (ids.reshape(REPLICAS, TOKENS * TOP)[..., None] == jnp.arange(EXPERTS, dtype=jnp.int32)).astype(jnp.float32)
        return jnp.einsum("rpe,rpd->ed", onehot, scaled)

    bias_grad = lax.map(backward_section, (upstream, gates_bwd, ids_bwd))
    return section_out, bias_grad
```

```python
import functools

import jax
import jax.numpy as jnp
from jax import lax
from jax.experimental import pallas as pl
from jax.experimental.pallas import tpu as pltpu
from jax.sharding import PartitionSpec as P

F32 = jnp.float32
BF16 = jnp.bfloat16
SIDE = 8
ROWS = 8
LANES = 128

CHUNKS = ((0, 384, "z"), (768, 384, "x"), (384, 384, "z"), (1152, 288, "x"))


def iota(shape, dim):
    return lax.broadcasted_iota(jnp.int32, shape, dim)


def dot(a, b, dims=((1,), (0,))):
    return lax.dot_general(a, b, (dims, ((), ())), preferred_element_type=F32)


def split(value):
    high = value.astype(BF16)
    return high, (value - high.astype(F32)).astype(BF16)


def table(ids, gates, owner):
    shape = owner.shape
    chosen, weight = jnp.zeros(shape, F32), jnp.zeros(shape, F32)
    for k in range(ids.shape[1]):
        hit = ids[:, k : k + 1] == owner
        chosen = jnp.where(hit, 1.0, chosen)
        weight = jnp.where(hit, gates[:, k : k + 1], weight)
    return chosen, weight


def combine_matrix(chosen, weight, cap, order):
    tokens, experts = chosen.shape
    slots = experts * cap
    earlier = (iota((tokens, tokens), 1) < iota((tokens, tokens), 0)).astype(F32).astype(BF16)
    rank = dot(earlier, chosen.astype(BF16))
    row, column = iota((experts, slots), 0), iota((experts, slots), 1)
    if order == "x":
        row = (row & (SIDE - 1)) * SIDE + (row >> (SIDE.bit_length() - 1))
    inside = column - row * cap
    member = (inside >= 0) & (inside < cap)
    spread = jnp.where(member, 1.0, 0.0).astype(BF16)
    slot = jnp.sum(jnp.where(member, inside, 0).astype(F32), axis=0, keepdims=True)
    hit = (dot(rank.astype(BF16), spread) == slot) & (dot(chosen.astype(BF16), spread) > 0.5)
    high, low = split(weight)
    parts = [jnp.where(hit, dot(part, spread), 0.0) for part in (high, low)]
    return jnp.concatenate(parts, axis=0).astype(BF16)


def kernel(
    cap,
    replicas,
    sections,
    carry,
    hidden,
    weight,
    bias,
    ids_fwd,
    gates_fwd,
    ids_bwd,
    gates_bwd,
    out,
    bias_grad,
    hid_v,
    wgt_v,
    inc_v,
    up_v,
    share,
    share_bf,
    share_in,
    col_out,
    col_in,
    row_out,
    row_in,
    *rest,
):
    n = len(CHUNKS)
    first_out, first_in, second_out, second_in = (rest[i * n : (i + 1) * n] for i in range(4))
    local_sem, send_sem, recv_sem = rest[4 * n :]
    me = lax.axis_index("expert")
    z, x = me // SIDE, me % SIDE
    sec, rep = lax.axis_index("section"), lax.axis_index("dp")
    tokens, width = inc_v.shape
    experts = SIDE * SIDE
    slots = experts * cap
    half = width // replicas
    group = SIDE * cap

    def along(axis, step):
        if axis == "z":
            other = (z + step) % SIDE
            return other, {"expert": other * SIDE + x}
        other = (x + step) % SIDE
        return other, {"expert": z * SIDE + other}

    after, before = (sec + 1) % sections, (sec + sections - 1) % sections

    barrier = pltpu.get_barrier_semaphore()
    partners = [along(axis, d)[1] for axis in "zx" for d in range(1, SIDE)]
    partners += [{"section": after}, {"section": before}, {"dp": 1 - rep}]
    for device in partners:
        pl.semaphore_signal(barrier, inc=1, device_id=device, device_id_type=pl.DeviceIdType.MESH)

    loads = [pltpu.make_async_copy(hidden.at[0, 0, 0], hid_v, local_sem.at[n])]
    for i, (start, size, _) in enumerate(CHUNKS):
        columns = pl.ds(start, size)
        loads.append(
            pltpu.make_async_copy(
                weight.at[0, 0, :, columns], wgt_v.at[:, columns], local_sem.at[i]
            )
        )
    for load in loads:
        load.start()

    def remote(src, dst, sem, device):
        return pltpu.make_async_remote_copy(
            src_ref=src,
            dst_ref=dst,
            send_sem=send_sem.at[sem],
            recv_sem=recv_sem.at[sem],
            device_id=device,
            device_id_type=pl.DeviceIdType.MESH,
        )

    def exchange(axis, src, dst, sem):
        here = z if axis == "z" else x
        copies = []
        for d in range(1, SIDE):
            other, device = along(axis, d)
            copy = remote(src.at[other], dst.at[here], sem + d - 1, device)
            copy.start()
            copies.append(copy)
        dst[here] = src[here]
        return copies

    def arrived(copies):
        for copy in copies:
            copy.wait_recv()

    swap_row, swap_col = iota((slots, slots), 0), iota((slots, slots), 1)
    low_group = sum((swap_row >= group * i).astype(jnp.int32) for i in range(1, SIDE))
    low_rest = swap_row - low_group * group
    inner = sum((low_rest >= cap * i).astype(jnp.int32) for i in range(1, SIDE))
    swap = swap_col == inner * group + low_group * cap + (low_rest - inner * cap)
    swap = jnp.where(swap, 1.0, 0.0).astype(BF16)
    owner = iota((tokens, experts), 1)
    chosen, gate = table(ids_fwd[0, 0], gates_fwd[0, 0], owner)
    combine = {order: combine_matrix(chosen, gate, cap, order) for order in "zx"}
    share[...] = jnp.zeros_like(share)

    def produce(i):
        start, size, axis = CHUNKS[i]
        columns = pl.ds(start, size)
        loads[i + 1].wait()
        block = dot(hid_v[...], wgt_v[:, columns]) + bias[0, :, columns].astype(F32)
        if axis == "x":
            block = dot(swap, block.astype(BF16))
        for other in range(SIDE):
            first_out[i][other] = block[other * group : (other + 1) * group].astype(BF16)

    def gathered(ref):
        return ref[...].reshape(slots, ref.shape[2])

    def turn(i):
        block = dot(swap, gathered(first_in[i]))
        for other in range(SIDE):
            second_out[i][other] = block[other * group : (other + 1) * group].astype(BF16)

    per = SIDE - 1
    first_sem = [i * per for i in range(n)]
    second_sem = [(n + i) * per for i in range(n)]
    col_sem, row_sem = 2 * n * per, (2 * n + 1) * per
    up_sem = (2 * n + 2) * per
    inc_sem, share_sem = up_sem + 1, up_sem + 2
    first, second = [None] * n, [None] * n
    other_axis = {"z": "x", "x": "z"}

    loads[0].wait()
    produce(0)
    pl.semaphore_wait(barrier, len(partners))
    first[0] = exchange(CHUNKS[0][2], first_out[0], first_in[0], first_sem[0])
    up_copy = remote(carry.at[0, 0], up_v, up_sem, {"section": before})
    up_copy.start()
    for i in range(1, n):
        produce(i)
        first[i] = exchange(CHUNKS[i][2], first_out[i], first_in[i], first_sem[i])

    owner = (owner & (SIDE - 1)) * SIDE + (owner >> (SIDE.bit_length() - 1))
    _, gate = table(ids_bwd[0, 0], gates_bwd[0, 0], owner)
    high, low = split(gate)
    up_copy.wait_recv()
    upstream = up_v[...]
    total = dot(high, upstream, ((0,), (0,))) + dot(low, upstream, ((0,), (0,)))
    for h in range(replicas):
        share[h, :, 0:half] = total[:, h * half : (h + 1) * half]
    share_bf[...] = share[1 - rep].astype(BF16)
    share_copy = remote(share_bf, share_in, share_sem, {"dp": 1 - rep})
    share_copy.start()
    inc_copy = remote(carry.at[1, 0], inc_v, inc_sem, {"section": after})
    inc_copy.start()

    def second_phase(i):
        arrived(first[i])
        turn(i)
        axis = other_axis[CHUNKS[i][2]]
        second[i] = exchange(axis, second_out[i], second_in[i], second_sem[i])

    second_phase(0)
    second_phase(1)

    share_copy.wait_recv()
    both = share[rep] + share_in[...].astype(F32)
    part = both.shape[1] // 2
    for other in range(SIDE):
        rows = both[other * SIDE : (other + 1) * SIDE]
        col_out[other] = jnp.concatenate([rows[:, :part], rows[:, part:]], axis=0).astype(BF16)
    col_copies = exchange("x", col_out, col_in, col_sem)

    for i in range(2, n):
        second_phase(i)

    arrived(col_copies)
    both = jnp.sum(col_in[...].astype(F32), axis=0)
    tiles = part // LANES
    for other in range(SIDE):
        for h in range(2):
            for tile in range(tiles):
                row_out[other, h * tiles + tile : h * tiles + tile + 1, :] = both[
                    h * SIDE + other : h * SIDE + other + 1, tile * LANES : (tile + 1) * LANES
                ]
    row_copies = exchange("z", row_out, row_in, row_sem)

    def finish(i):
        start, size, axis = CHUNKS[i]
        arrived(second[i])
        mixed = dot(combine[other_axis[axis]], gathered(second_in[i]))
        mixed = mixed[:tokens] + mixed[tokens:] + inc_v[:, start : start + size].astype(F32)
        out[0, 0, :, start : start + size] = mixed.astype(BF16)

    inc_copy.wait_recv()
    finish(0)
    finish(1)
    arrived(row_copies)
    mine = jnp.sum(row_in[...], axis=0)
    for tile in range(pl.cdiv(half, LANES)):
        size = min(LANES, half - tile * LANES)
        bias_grad[0, :, tile * LANES : tile * LANES + size] = mine[tile : tile + 1, :size]
    for i in range(2, n):
        finish(i)

    copies = [up_copy, inc_copy, share_copy, *col_copies, *row_copies]
    for group_of in first + second:
        copies += group_of
    for copy in copies:
        copy.wait_send()


def solution(mesh):
    sections, replicas = mesh.shape["section"], mesh.shape["dp"]

    def step(carry, hidden, weight, bias, ids_fwd, gates_fwd, ids_bwd, gates_bwd):
        tokens, width = carry.shape[2:]
        slots, depth = hidden.shape[3:]
        experts = mesh.shape["expert"]
        cap = slots // experts
        half = width // replicas
        wide = pl.cdiv(half, 2 * LANES) * 2 * LANES
        blocks = [pltpu.VMEM((SIDE, SIDE * cap, size), BF16) for _, size, _ in CHUNKS]
        messages = (2 * len(CHUNKS) + 2) * (SIDE - 1) + 3
        in_hbm, in_vmem = pl.BlockSpec(memory_space=pl.ANY), pl.BlockSpec(memory_space=pltpu.VMEM)
        return pl.pallas_call(
            functools.partial(kernel, cap, replicas, sections),
            out_shape=(
                jax.ShapeDtypeStruct((1, 1, tokens, width), BF16),
                jax.ShapeDtypeStruct((1, 1, half), F32),
            ),
            in_specs=[in_hbm] * 3 + [in_vmem] * 5,
            out_specs=(in_vmem, in_vmem),
            scratch_shapes=[
                pltpu.VMEM((slots, depth), BF16),
                pltpu.VMEM((depth, width), BF16),
                pltpu.VMEM((tokens, width), BF16),
                pltpu.VMEM((tokens, width), BF16),
                pltpu.VMEM((replicas, experts, wide), F32),
                pltpu.VMEM((experts, wide), BF16),
                pltpu.VMEM((experts, wide), BF16),
                pltpu.VMEM((SIDE, 2 * SIDE, wide // 2), BF16),
                pltpu.VMEM((SIDE, 2 * SIDE, wide // 2), BF16),
                pltpu.VMEM((SIDE, ROWS, LANES), F32),
                pltpu.VMEM((SIDE, ROWS, LANES), F32),
                *(blocks * 4),
                pltpu.SemaphoreType.DMA((len(CHUNKS) + 1,)),
                pltpu.SemaphoreType.DMA((messages,)),
                pltpu.SemaphoreType.DMA((messages,)),
            ],
            compiler_params=pltpu.CompilerParams(
                collective_id=0, has_side_effects=True, vmem_limit_bytes=48 * 2**20
            ),
            cost_estimate=pl.CostEstimate(
                flops=2 * slots * depth * width,
                bytes_accessed=2 * (depth * width + slots * depth + 4 * tokens * width),
                transcendentals=0,
            ),
        )(carry, hidden, weight, bias, ids_fwd, gates_fwd, ids_bwd, gates_bwd)

    placed = (
        P("section", "dp", "expert", None),
        P("section", "dp", "expert", None, None),
        P("section", "expert", None, None),
        P("section", "expert", None),
        P("section", "dp", "expert", None),
        P("section", "dp", "expert", None),
        P("section", "dp", "expert", None),
        P("section", "dp", "expert", None),
    )
    return jax.shard_map(
        step,
        mesh=mesh,
        in_specs=placed,
        out_specs=(P("section", "dp", "expert", None), P("section", "expert", "dp")),
        check_vma=False,
    )
```

```python
import functools

import jax
import jax.numpy as jnp
from jax import lax
from jax.experimental import pallas as pl
from jax.experimental.pallas import tpu as pltpu
from jax.sharding import PartitionSpec as P

F32 = jnp.float32
BF16 = jnp.bfloat16
SIDE = 8
ROWS = 8
LANES = 128

CHUNKS = (
    (0, 256, "z"),
    (768, 256, "x"),
    (256, 256, "z"),
    (1024, 256, "x"),
    (512, 256, "z"),
    (1280, 160, "x"),
)


def iota(shape, dim):
    return lax.broadcasted_iota(jnp.int32, shape, dim)


def dot(a, b, dims=((1,), (0,))):
    return lax.dot_general(a, b, (dims, ((), ())), preferred_element_type=F32)


def swapped(expert):
    return (expert & (SIDE - 1)) * SIDE + (expert >> (SIDE.bit_length() - 1))


def split(value):
    high = value.astype(BF16)
    return high, (value - high.astype(F32)).astype(BF16)


def table(ids, gates, owner):
    shape = owner.shape
    chosen, weight = jnp.zeros(shape, F32), jnp.zeros(shape, F32)
    for k in range(ids.shape[0]):
        hit = ids[k : k + 1] == owner
        chosen = jnp.where(hit, 1.0, chosen)
        weight = jnp.where(hit, gates[k : k + 1], weight)
    return chosen, weight


def combine_matrix(chosen, weight, cap, order):
    experts, tokens = chosen.shape
    slots = experts * cap
    earlier = (iota((tokens, tokens), 0) < iota((tokens, tokens), 1)).astype(F32).astype(BF16)
    rank = dot(chosen.astype(BF16), earlier)
    row, column = iota((experts, slots), 0), iota((experts, slots), 1)
    if order == "x":
        row = swapped(row)
    inside = column - row * cap
    member = (inside >= 0) & (inside < cap)
    spread = jnp.where(member, 1.0, 0.0).astype(BF16)
    slot = jnp.sum(jnp.where(member, inside, 0).astype(F32), axis=0, keepdims=True)

    def widen(part):
        return dot(part.astype(BF16), spread, ((0,), (0,)))

    hit = (widen(rank) == slot) & (widen(chosen) > 0.5)
    parts = [jnp.where(hit, widen(part), 0.0) for part in split(weight)]
    return jnp.concatenate(parts, axis=0).astype(BF16)


def kernel(
    cap,
    replicas,
    sections,
    carry,
    hidden,
    weight,
    bias,
    ids_fwd,
    gates_fwd,
    ids_bwd,
    gates_bwd,
    out_to,
    bias_to,
    out,
    bias_grad,
    hid_v,
    wgt_v,
    bias_v,
    ids_v,
    gates_v,
    inc_v,
    grad_v,
    grad_out,
    grad_in,
    peer_ids,
    peer_gates,
    col_out,
    col_in,
    row_out,
    row_in,
    *rest,
):
    n = len(CHUNKS)
    first_out, first_in, second_out, second_in = (rest[i * n : (i + 1) * n] for i in range(4))
    local_sem, store_sem, send_sem, recv_sem = rest[4 * n :]
    me = lax.axis_index("expert")
    z, x = me // SIDE, me % SIDE
    sec, rep = lax.axis_index("section"), lax.axis_index("dp")
    tokens, width = inc_v.shape
    experts = SIDE * SIDE
    slots = experts * cap
    half = width // replicas
    group = SIDE * cap

    def along(axis, step):
        if axis == "z":
            other = (z + step) % SIDE
            return other, {"expert": other * SIDE + x}
        other = (x + step) % SIDE
        return other, {"expert": z * SIDE + other}

    after, before = (sec + 1) % sections, (sec + sections - 1) % sections

    barrier = pltpu.get_barrier_semaphore()
    partners = [along(axis, d)[1] for axis in "zx" for d in range(1, SIDE)]
    other_rep = {"dp": 1 - rep}
    partners += [{"section": s} | d for s in (after, before) for d in ({}, other_rep)]
    partners += [other_rep]
    for device in partners:
        pl.semaphore_signal(barrier, inc=1, device_id=device, device_id_type=pl.DeviceIdType.MESH)

    loads = [pltpu.make_async_copy(hidden.at[0, 0, 0], hid_v, local_sem.at[n])]
    small = [
        pltpu.make_async_copy(src.at[at], dst, local_sem.at[n + 1 + i])
        for i, (src, at, dst) in enumerate(
            (
                (bias, 0, bias_v),
                (carry, (0, 0), grad_v),
                (ids_fwd, (0, 0), ids_v.at[0]),
                (ids_bwd, (0, 0), ids_v.at[1]),
                (gates_fwd, (0, 0), gates_v.at[0]),
                (gates_bwd, (0, 0), gates_v.at[1]),
            )
        )
    ]
    for i, (start, size, _) in enumerate(CHUNKS):
        columns = pl.ds(start, size)
        loads.append(
            pltpu.make_async_copy(
                weight.at[0, 0, :, columns], wgt_v.at[:, columns], local_sem.at[i]
            )
        )
    for load in small[:2] + loads[:2] + small[2:] + loads[2:]:
        load.start()

    def remote(src, dst, sem, device):
        return pltpu.make_async_remote_copy(
            src_ref=src,
            dst_ref=dst,
            send_sem=send_sem.at[sem],
            recv_sem=recv_sem.at[sem],
            device_id=device,
            device_id_type=pl.DeviceIdType.MESH,
        )

    def exchange(axis, src, dst, sem):
        here = z if axis == "z" else x
        copies = []
        for d in farthest_first:
            other, device = along(axis, d)
            copy = remote(src.at[other], dst.at[here], sem + d - 1, device)
            copy.start()
            copies.append(copy)
        dst[here] = src[here]
        return copies

    farthest_first = sorted(range(1, SIDE), key=lambda d: -min(d, SIDE - d))

    @jax.named_scope("arrive")
    def arrived(copies):
        for copy in copies:
            copy.wait_recv()

    swap_row, swap_col = iota((slots, slots), 0), iota((slots, slots), 1)
    low_group = sum((swap_row >= group * i).astype(jnp.int32) for i in range(1, SIDE))
    low_rest = swap_row - low_group * group
    inner = sum((low_rest >= cap * i).astype(jnp.int32) for i in range(1, SIDE))
    swap = swap_col == inner * group + low_group * cap + (low_rest - inner * cap)
    swap = jnp.where(swap, 1.0, 0.0).astype(BF16)

    @jax.named_scope("produce")
    def produce(i):
        start, size, axis = CHUNKS[i]
        columns = pl.ds(start, size)
        loads[i + 1].wait()
        block = dot(hid_v[...], wgt_v[:, columns]) + bias_v[:, columns].astype(F32)
        if axis == "x":
            block = dot(swap, block.astype(BF16))
        for other in range(SIDE):
            first_out[i][other] = block[other * group : (other + 1) * group].astype(BF16)

    def gathered(ref):
        return ref[...].reshape(slots, ref.shape[2])

    @jax.named_scope("turn")
    def turn(i):
        block = dot(swap, gathered(first_in[i]))
        for other in range(SIDE):
            second_out[i][other] = block[other * group : (other + 1) * group].astype(BF16)

    per = SIDE - 1
    first_sem = [i * per for i in range(n)]
    second_sem = [(n + i) * per for i in range(n)]
    col_sem, row_sem = 2 * n * per, (2 * n + 1) * per
    up_sem = (2 * n + 2) * per
    inc_sem = up_sem + 4
    first, second = [None] * n, [None] * n
    other_axis = {"z": "x", "x": "z"}

    small[1].wait()
    for h in range(replicas):
        part = grad_v[:, h * half : (h + 1) * half]
        blank = jnp.zeros((tokens, grad_out.shape[2] - half), BF16)
        grad_out[h] = jnp.concatenate([part, blank], axis=1)
    loads[0].wait()
    small[0].wait()
    produce(0)
    with jax.named_scope("greet"):
        pl.semaphore_wait(barrier, len(partners))
    grad_copies = [
        remote(grad_out.at[1 - rep], grad_in.at[1], up_sem + 1, {"section": before} | other_rep),
        remote(grad_out.at[rep], grad_in.at[0], up_sem, {"section": before}),
        remote(ids_bwd.at[0, 0], peer_ids, up_sem + 2, other_rep),
        remote(gates_bwd.at[0, 0], peer_gates, up_sem + 3, other_rep),
    ]
    for copy in grad_copies:
        copy.start()
    first[0] = exchange(CHUNKS[0][2], first_out[0], first_in[0], first_sem[0])
    for i in range(1, n):
        produce(i)
        first[i] = exchange(CHUNKS[i][2], first_out[i], first_in[i], first_sem[i])

    for load in small[2:]:
        load.wait()
    owner = iota((experts, tokens), 0)
    with jax.named_scope("upstream"):
        arrived(grad_copies)
    inc_copy = remote(carry.at[1, 0], inc_v, inc_sem, {"section": after})
    inc_copy.start()
    total = jnp.zeros((experts, grad_in.shape[2]), F32)
    for i, (ids, gates) in enumerate(((ids_v[1], gates_v[1]), (peer_ids[...], peer_gates[...]))):
        _, gate = table(ids, gates, swapped(owner))
        for part in split(gate):
            total = total + dot(part, grad_in[i])
    part = total.shape[1] // 2
    for other in range(SIDE):
        rows = total[other * SIDE : (other + 1) * SIDE]
        col_out[other] = jnp.concatenate([rows[:, :part], rows[:, part:]], axis=0).astype(BF16)
    col_copies = exchange("x", col_out, col_in, col_sem)

    chosen, gate = table(ids_v[0], gates_v[0], owner)
    combine = {order: combine_matrix(chosen, gate, cap, order) for order in "zx"}

    def second_phase(i):
        arrived(first[i])
        turn(i)
        axis = other_axis[CHUNKS[i][2]]
        second[i] = exchange(axis, second_out[i], second_in[i], second_sem[i])

    for i in range(n):
        second_phase(i)

    arrived(col_copies)
    both = jnp.sum(col_in[...].astype(F32), axis=0)
    tiles = part // LANES
    for other in range(SIDE):
        for h in range(2):
            for tile in range(tiles):
                row_out[other, h * tiles + tile : h * tiles + tile + 1, :] = both[
                    h * SIDE + other : h * SIDE + other + 1, tile * LANES : (tile + 1) * LANES
                ]
    row_copies = exchange("z", row_out, row_in, row_sem)

    @jax.named_scope("finish")
    def finish(i):
        start, size, axis = CHUNKS[i]
        arrived(second[i])
        mixed = dot(combine[other_axis[axis]], gathered(second_in[i]))
        mixed = mixed[:tokens] + mixed[tokens:] + inc_v[:, start : start + size].astype(F32)
        out[:, start : start + size] = mixed.astype(BF16)
        store = pltpu.make_async_copy(
            out.at[:, pl.ds(start, size)], out_to.at[0, 0, :, pl.ds(start, size)], store_sem.at[i]
        )
        store.start()
        return store

    inc_copy.wait_recv()
    stores = [finish(i) for i in range(n)]
    arrived(row_copies)
    mine = jnp.sum(row_in[...], axis=0)
    for tile in range(pl.cdiv(half, LANES)):
        size = min(LANES, half - tile * LANES)
        bias_grad[:, tile * LANES : tile * LANES + size] = mine[tile : tile + 1, :size]
    stores.append(pltpu.make_async_copy(bias_grad, bias_to.at[0], store_sem.at[n]))
    stores[n].start()
    copies = [inc_copy, *grad_copies, *col_copies, *row_copies]
    for group_of in first + second:
        copies += group_of
    for copy in copies:
        copy.wait_send()
    for store in stores:
        store.wait()


def hand_over(out, bias_grad, out_to, bias_to, out_v, bias_v, sem):
    steps = [
        (pltpu.make_async_copy(a, v, sem.at[2 * i]), pltpu.make_async_copy(v, b, sem.at[2 * i + 1]))
        for i, (a, v, b) in enumerate(((out, out_v, out_to), (bias_grad, bias_v, bias_to)))
    ]
    for load, _ in steps:
        load.start()
    for load, store in steps:
        load.wait()
        store.start()
    for _, store in steps:
        store.wait()


def solution(mesh):
    sections, replicas = mesh.shape["section"], mesh.shape["dp"]

    def step(carry, hidden, weight, bias, ids_fwd, gates_fwd, ids_bwd, gates_bwd):
        tokens, width = carry.shape[2:]
        slots, depth = hidden.shape[3:]
        experts = mesh.shape["expert"]
        cap = slots // experts
        half = width // replicas
        wide = pl.cdiv(half, 2 * LANES) * 2 * LANES
        blocks = [pltpu.VMEM((SIDE, SIDE * cap, size), BF16) for _, size, _ in CHUNKS]
        messages = (2 * len(CHUNKS) + 2) * (SIDE - 1) + 5
        in_hbm = pl.BlockSpec(memory_space=pltpu.HBM)
        shapes = (
            jax.ShapeDtypeStruct((1, 1, tokens, width), BF16),
            jax.ShapeDtypeStruct((1, 1, half), F32),
        )
        results = pl.pallas_call(
            functools.partial(kernel, cap, replicas, sections),
            out_shape=shapes,
            in_specs=[in_hbm] * 8,
            out_specs=(in_hbm, in_hbm),
            scratch_shapes=[
                pltpu.VMEM((tokens, width), BF16),
                pltpu.VMEM((1, half), F32),
                pltpu.VMEM((slots, depth), BF16),
                pltpu.VMEM((depth, width), BF16),
                pltpu.VMEM((1, width), BF16),
                pltpu.VMEM((2,) + ids_fwd.shape[3:1:-1], jnp.int32),
                pltpu.VMEM((2,) + ids_fwd.shape[3:1:-1], F32),
                pltpu.VMEM((tokens, width), BF16),
                pltpu.VMEM((tokens, width), BF16),
                pltpu.VMEM((replicas, tokens, wide), BF16),
                pltpu.VMEM((replicas, tokens, wide), BF16),
                pltpu.VMEM(ids_fwd.shape[3:1:-1], jnp.int32),
                pltpu.VMEM(ids_fwd.shape[3:1:-1], F32),
                pltpu.VMEM((SIDE, 2 * SIDE, wide // 2), BF16),
                pltpu.VMEM((SIDE, 2 * SIDE, wide // 2), BF16),
                pltpu.VMEM((SIDE, ROWS, LANES), F32),
                pltpu.VMEM((SIDE, ROWS, LANES), F32),
                *(blocks * 4),
                pltpu.SemaphoreType.DMA((len(CHUNKS) + 7,)),
                pltpu.SemaphoreType.DMA((len(CHUNKS) + 1,)),
                pltpu.SemaphoreType.DMA((messages,)),
                pltpu.SemaphoreType.DMA((messages,)),
            ],
            compiler_params=pltpu.CompilerParams(
                collective_id=0, has_side_effects=True, vmem_limit_bytes=64 * 2**20
            ),
            cost_estimate=pl.CostEstimate(
                flops=2 * slots * depth * width,
                bytes_accessed=2 * (depth * width + slots * depth + 4 * tokens * width),
                transcendentals=0,
            ),
        )(
            carry,
            hidden,
            weight,
            bias,
            *(jnp.swapaxes(a, 2, 3) for a in (ids_fwd, gates_fwd, ids_bwd, gates_bwd)),
        )
        anywhere = pl.BlockSpec(memory_space=pl.ANY)
        return pl.pallas_call(
            hand_over,
            out_shape=shapes,
            in_specs=[anywhere] * 2,
            out_specs=(anywhere, anywhere),
            scratch_shapes=[
                *(pltpu.VMEM(shape.shape, shape.dtype) for shape in shapes),
                pltpu.SemaphoreType.DMA((4,)),
            ],
            compiler_params=pltpu.CompilerParams(vmem_limit_bytes=64 * 2**20),
        )(*results)

    placed = (
        P("section", "dp", "expert", None),
        P("section", "dp", "expert", None, None),
        P("section", "expert", None, None),
        P("section", "expert", None),
        P("section", "dp", "expert", None),
        P("section", "dp", "expert", None),
        P("section", "dp", "expert", None),
        P("section", "dp", "expert", None),
    )
    return jax.shard_map(
        step,
        mesh=mesh,
        in_specs=placed,
        out_specs=(P("section", "dp", "expert", None), P("section", "expert", "dp")),
        check_vma=False,
    )
```

```python
import functools

import jax
import jax.numpy as jnp
from jax import lax
from jax.experimental import pallas as pl
from jax.experimental.pallas import tpu as pltpu
from jax.sharding import PartitionSpec as P

F32 = jnp.float32
BF16 = jnp.bfloat16
SIDE = 8
ROWS = 8
LANES = 128

CHUNKS = (
    (768, 512, "x"),
    (0, 384, "z"),
    (1280, 160, "x"),
    (384, 384, "z"),
)

TAIL = 32
PARTS = LANES // TAIL


def packed_rows(group):
    return pl.cdiv(group // PARTS, 16) * 16


def block_shape(group, size):
    if size % LANES == 0:
        return (group, size)
    assert size == LANES + TAIL
    return (packed_rows(group) + group, LANES)


def iota(shape, dim):
    return lax.broadcasted_iota(jnp.int32, shape, dim)


def dot(a, b, dims=((1,), (0,))):
    return lax.dot_general(a, b, (dims, ((), ())), preferred_element_type=F32)


def swapped(expert):
    return (expert & (SIDE - 1)) * SIDE + (expert >> (SIDE.bit_length() - 1))


def split(value):
    high = value.astype(BF16)
    return high, (value - high.astype(F32)).astype(BF16)


def table(ids, gates, owner):
    shape = owner.shape
    chosen, weight = jnp.zeros(shape, F32), jnp.zeros(shape, F32)
    for k in range(ids.shape[0]):
        hit = ids[k : k + 1] == owner
        chosen = jnp.where(hit, 1.0, chosen)
        weight = jnp.where(hit, gates[k : k + 1], weight)
    return chosen, weight


def combine_matrix(chosen, weight, cap, order):
    experts, tokens = chosen.shape
    slots = experts * cap
    earlier = (iota((tokens, tokens), 0) < iota((tokens, tokens), 1)).astype(F32).astype(BF16)
    rank = dot(chosen.astype(BF16), earlier)
    row, column = iota((experts, slots), 0), iota((experts, slots), 1)
    if order == "x":
        row = swapped(row)
    inside = column - row * cap
    member = (inside >= 0) & (inside < cap)
    spread = jnp.where(member, 1.0, 0.0).astype(BF16)
    slot = jnp.sum(jnp.where(member, inside, 0).astype(F32), axis=0, keepdims=True)

    def widen(part):
        return dot(part.astype(BF16), spread, ((0,), (0,)))

    hit = (widen(rank) == slot) & (widen(chosen) > 0.5)
    parts = [jnp.where(hit, widen(part), 0.0) for part in split(weight)]
    return jnp.concatenate(parts, axis=0).astype(BF16)


def kernel(
    cap,
    replicas,
    sections,
    carry,
    hidden,
    weight,
    bias,
    ids_fwd,
    gates_fwd,
    ids_bwd,
    gates_bwd,
    out_to,
    bias_to,
    out,
    bias_grad,
    hid_v,
    wgt_v,
    bias_v,
    ids_v,
    gates_v,
    inc_v,
    grad_v,
    grad_out,
    grad_in,
    peer_ids,
    peer_gates,
    col_out,
    col_in,
    row_out,
    row_in,
    *rest,
):
    n = len(CHUNKS)
    first_out, first_in, second_out, second_in = (rest[i * n : (i + 1) * n] for i in range(4))
    local_sem, store_sem, send_sem, recv_sem = rest[4 * n :]
    me = lax.axis_index("expert")
    z, x = me // SIDE, me % SIDE
    sec, rep = lax.axis_index("section"), lax.axis_index("dp")
    tokens, width = inc_v.shape
    experts = SIDE * SIDE
    slots = experts * cap
    half = width // replicas
    group = SIDE * cap

    def along(axis, step):
        if axis == "z":
            other = (z + step) % SIDE
            return other, {"expert": other * SIDE + x}
        other = (x + step) % SIDE
        return other, {"expert": z * SIDE + other}

    after, before = (sec + 1) % sections, (sec + sections - 1) % sections

    barrier = pltpu.get_barrier_semaphore()
    partners = [along(axis, d)[1] for axis in "zx" for d in range(1, SIDE)]
    other_rep = {"dp": 1 - rep}
    partners += [{"section": s} | d for s in (after, before) for d in ({}, other_rep)]
    partners += [other_rep]
    for device in partners:
        pl.semaphore_signal(barrier, inc=1, device_id=device, device_id_type=pl.DeviceIdType.MESH)

    loads = [pltpu.make_async_copy(hidden.at[0, 0, 0], hid_v, local_sem.at[n])]
    small = [
        pltpu.make_async_copy(src.at[at], dst, local_sem.at[n + 1 + i])
        for i, (src, at, dst) in enumerate(
            (
                (bias, 0, bias_v),
                (carry, (0, 0), grad_v),
                (ids_fwd, (0, 0), ids_v.at[0]),
                (ids_bwd, (0, 0), ids_v.at[1]),
                (gates_fwd, (0, 0), gates_v.at[0]),
                (gates_bwd, (0, 0), gates_v.at[1]),
            )
        )
    ]
    for i, (start, size, _) in enumerate(CHUNKS):
        columns = pl.ds(start, size)
        loads.append(
            pltpu.make_async_copy(
                weight.at[0, 0, :, columns], wgt_v.at[:, columns], local_sem.at[i]
            )
        )
    for load in small[:2] + loads[:2] + small[2:] + loads[2:]:
        load.start()

    def remote(src, dst, sem, device):
        return pltpu.make_async_remote_copy(
            src_ref=src,
            dst_ref=dst,
            send_sem=send_sem.at[sem],
            recv_sem=recv_sem.at[sem],
            device_id=device,
            device_id_type=pl.DeviceIdType.MESH,
        )

    def exchange(axis, src, dst, sem):
        here = z if axis == "z" else x
        copies = []
        for d in farthest_first:
            other, device = along(axis, d)
            copy = remote(src.at[other], dst.at[here], sem + d - 1, device)
            copy.start()
            copies.append(copy)
        dst[here] = src[here]
        return copies

    farthest_first = sorted(range(1, SIDE), key=lambda d: -min(d, SIDE - d))

    @jax.named_scope("arrive")
    def arrived(copies):
        for copy in copies:
            copy.wait_recv()

    swap_row, swap_col = iota((slots, slots), 0), iota((slots, slots), 1)
    low_group = sum((swap_row >= group * i).astype(jnp.int32) for i in range(1, SIDE))
    low_rest = swap_row - low_group * group
    inner = sum((low_rest >= cap * i).astype(jnp.int32) for i in range(1, SIDE))
    swap = swap_col == inner * group + low_group * cap + (low_rest - inner * cap)
    swap = jnp.where(swap, 1.0, 0.0).astype(BF16)

    @jax.named_scope("produce")
    def produce(i):
        start, size, axis = CHUNKS[i]
        columns = pl.ds(start, size)
        loads[i + 1].wait()
        block = dot(hid_v[...], wgt_v[:, columns]) + bias_v[:, columns].astype(F32)
        if axis == "x":
            block = dot(swap, block.astype(BF16))
        put(first_out[i], block)

    tall, short = packed_rows(group), group // PARTS

    def picks():
        row, column = iota((SIDE * tall, slots), 0), iota((SIDE * tall, slots), 1)
        inside = row & (tall - 1)
        at = (row >> (tall.bit_length() - 1)) * group + inside
        inside = inside < short
        return [jnp.where(inside & (column == at + q * short), 1.0, 0.0).astype(BF16) for q in range(PARTS)]

    pick = picks()

    def put(ref, block):
        whole = ref.shape[2]
        above = ref.shape[1] - group
        block = block.astype(BF16)
        if above:
            packed = jnp.concatenate([dot(p, block[:, whole:]) for p in pick], axis=1).astype(BF16)
        for other in range(SIDE):
            ref[other, above:, :] = block[other * group : (other + 1) * group, :whole]
            if above:
                ref[other, :above, :] = packed[other * above : (other + 1) * above]

    def gathered(ref):
        above = ref.shape[1] - group
        rows = ref[:, above:, :].reshape(slots, ref.shape[2])
        if not above:
            return rows
        packed = ref[:, :above, :].reshape(SIDE * above, ref.shape[2])
        tail = jnp.zeros((slots, TAIL), F32)
        for q, p in enumerate(pick):
            tail = tail + dot(p, packed[:, q * TAIL : (q + 1) * TAIL], ((0,), (0,)))
        return jnp.concatenate([rows, tail.astype(BF16)], axis=1)

    @jax.named_scope("turn")
    def turn(i):
        put(second_out[i], dot(swap, gathered(first_in[i])))

    per = SIDE - 1
    first_sem = [i * per for i in range(n)]
    second_sem = [(n + i) * per for i in range(n)]
    col_sem, row_sem = 2 * n * per, (2 * n + 1) * per
    up_sem = (2 * n + 2) * per
    inc_sem = up_sem + 4
    first, second = [None] * n, [None] * n
    other_axis = {"z": "x", "x": "z"}

    small[1].wait()
    for h in range(replicas):
        part = grad_v[:, h * half : (h + 1) * half]
        blank = jnp.zeros((tokens, grad_out.shape[2] - half), BF16)
        grad_out[h] = jnp.concatenate([part, blank], axis=1)
    loads[0].wait()
    small[0].wait()
    produce(0)
    with jax.named_scope("greet"):
        pl.semaphore_wait(barrier, len(partners))
    grad_copies = [
        remote(grad_out.at[1 - rep], grad_in.at[1], up_sem + 1, {"section": before} | other_rep),
        remote(grad_out.at[rep], grad_in.at[0], up_sem, {"section": before}),
        remote(ids_bwd.at[0, 0], peer_ids, up_sem + 2, other_rep),
        remote(gates_bwd.at[0, 0], peer_gates, up_sem + 3, other_rep),
    ]
    for copy in grad_copies:
        copy.start()
    first[0] = exchange(CHUNKS[0][2], first_out[0], first_in[0], first_sem[0])
    for i in range(1, n):
        produce(i)
        first[i] = exchange(CHUNKS[i][2], first_out[i], first_in[i], first_sem[i])

    for load in small[2:]:
        load.wait()
    owner = iota((experts, tokens), 0)
    with jax.named_scope("upstream"):
        arrived(grad_copies)
    inc_copy = remote(carry.at[1, 0], inc_v, inc_sem, {"section": after})
    inc_copy.start()
    total = jnp.zeros((experts, grad_in.shape[2]), F32)
    for i, (ids, gates) in enumerate(((ids_v[1], gates_v[1]), (peer_ids[...], peer_gates[...]))):
        _, gate = table(ids, gates, swapped(owner))
        for part in split(gate):
            total = total + dot(part, grad_in[i])
    part = total.shape[1] // 2
    for other in range(SIDE):
        rows = total[other * SIDE : (other + 1) * SIDE]
        col_out[other] = jnp.concatenate([rows[:, :part], rows[:, part:]], axis=0).astype(BF16)
    col_copies = exchange("x", col_out, col_in, col_sem)

    chosen, gate = table(ids_v[0], gates_v[0], owner)
    combine = {order: combine_matrix(chosen, gate, cap, order) for order in "zx"}

    def second_phase(i):
        arrived(first[i])
        turn(i)
        axis = other_axis[CHUNKS[i][2]]
        second[i] = exchange(axis, second_out[i], second_in[i], second_sem[i])

    for i in range(n - 2):
        second_phase(i)

    arrived(col_copies)
    both = jnp.sum(col_in[...].astype(F32), axis=0)
    tiles = part // LANES
    for other in range(SIDE):
        for h in range(2):
            for tile in range(tiles):
                row_out[other, h * tiles + tile : h * tiles + tile + 1, :] = both[
                    h * SIDE + other : h * SIDE + other + 1, tile * LANES : (tile + 1) * LANES
                ]
    row_copies = exchange("z", row_out, row_in, row_sem)

    for i in range(n - 2, n):
        second_phase(i)

    @jax.named_scope("finish")
    def finish(i):
        start, size, axis = CHUNKS[i]
        arrived(second[i])
        mixed = dot(combine[other_axis[axis]], gathered(second_in[i]))
        mixed = mixed[:tokens] + mixed[tokens:] + inc_v[:, start : start + size].astype(F32)
        out[:, start : start + size] = mixed.astype(BF16)
        store = pltpu.make_async_copy(
            out.at[:, pl.ds(start, size)], out_to.at[0, 0, :, pl.ds(start, size)], store_sem.at[i]
        )
        store.start()
        return store

    inc_copy.wait_recv()
    stores = [finish(i) for i in range(n)]
    arrived(row_copies)
    mine = jnp.sum(row_in[...], axis=0)
    for tile in range(pl.cdiv(half, LANES)):
        size = min(LANES, half - tile * LANES)
        bias_grad[:, tile * LANES : tile * LANES + size] = mine[tile : tile + 1, :size]
    stores.append(pltpu.make_async_copy(bias_grad, bias_to.at[0], store_sem.at[n]))
    stores[n].start()
    copies = [inc_copy, *grad_copies, *col_copies, *row_copies]
    for group_of in first + second:
        copies += group_of
    for copy in copies:
        copy.wait_send()
    for store in stores:
        store.wait()


def hand_over(out, bias_grad, out_to, bias_to, out_v, bias_v, sem):
    steps = [
        (pltpu.make_async_copy(a, v, sem.at[2 * i]), pltpu.make_async_copy(v, b, sem.at[2 * i + 1]))
        for i, (a, v, b) in enumerate(((out, out_v, out_to), (bias_grad, bias_v, bias_to)))
    ]
    for load, _ in steps:
        load.start()
    for load, store in steps:
        load.wait()
        store.start()
    for _, store in steps:
        store.wait()


def solution(mesh):
    sections, replicas = mesh.shape["section"], mesh.shape["dp"]

    def step(carry, hidden, weight, bias, ids_fwd, gates_fwd, ids_bwd, gates_bwd):
        tokens, width = carry.shape[2:]
        slots, depth = hidden.shape[3:]
        experts = mesh.shape["expert"]
        cap = slots // experts
        half = width // replicas
        wide = pl.cdiv(half, 2 * LANES) * 2 * LANES
        blocks = [
            pltpu.VMEM((SIDE,) + block_shape(SIDE * cap, size), BF16) for _, size, _ in CHUNKS
        ]
        messages = (2 * len(CHUNKS) + 2) * (SIDE - 1) + 5
        in_hbm = pl.BlockSpec(memory_space=pltpu.HBM)
        shapes = (
            jax.ShapeDtypeStruct((1, 1, tokens, width), BF16),
            jax.ShapeDtypeStruct((1, 1, half), F32),
        )
        results = pl.pallas_call(
            functools.partial(kernel, cap, replicas, sections),
            out_shape=shapes,
            in_specs=[in_hbm] * 8,
            out_specs=(in_hbm, in_hbm),
            scratch_shapes=[
                pltpu.VMEM((tokens, width), BF16),
                pltpu.VMEM((1, half), F32),
                pltpu.VMEM((slots, depth), BF16),
                pltpu.VMEM((depth, width), BF16),
                pltpu.VMEM((1, width), BF16),
                pltpu.VMEM((2,) + ids_fwd.shape[3:1:-1], jnp.int32),
                pltpu.VMEM((2,) + ids_fwd.shape[3:1:-1], F32),
                pltpu.VMEM((tokens, width), BF16),
                pltpu.VMEM((tokens, width), BF16),
                pltpu.VMEM((replicas, tokens, wide), BF16),
                pltpu.VMEM((replicas, tokens, wide), BF16),
                pltpu.VMEM(ids_fwd.shape[3:1:-1], jnp.int32),
                pltpu.VMEM(ids_fwd.shape[3:1:-1], F32),
                pltpu.VMEM((SIDE, 2 * SIDE, wide // 2), BF16),
                pltpu.VMEM((SIDE, 2 * SIDE, wide // 2), BF16),
                pltpu.VMEM((SIDE, ROWS, LANES), F32),
                pltpu.VMEM((SIDE, ROWS, LANES), F32),
                *(blocks * 4),
                pltpu.SemaphoreType.DMA((len(CHUNKS) + 7,)),
                pltpu.SemaphoreType.DMA((len(CHUNKS) + 1,)),
                pltpu.SemaphoreType.DMA((messages,)),
                pltpu.SemaphoreType.DMA((messages,)),
            ],
            compiler_params=pltpu.CompilerParams(
                collective_id=0, has_side_effects=True, vmem_limit_bytes=64 * 2**20
            ),
            cost_estimate=pl.CostEstimate(
                flops=2 * slots * depth * width,
                bytes_accessed=2 * (depth * width + slots * depth + 4 * tokens * width),
                transcendentals=0,
            ),
        )(
            carry,
            hidden,
            weight,
            bias,
            *(jnp.swapaxes(a, 2, 3) for a in (ids_fwd, gates_fwd, ids_bwd, gates_bwd)),
        )
        anywhere = pl.BlockSpec(memory_space=pl.ANY)
        return pl.pallas_call(
            hand_over,
            out_shape=shapes,
            in_specs=[anywhere] * 2,
            out_specs=(anywhere, anywhere),
            scratch_shapes=[
                *(pltpu.VMEM(shape.shape, shape.dtype) for shape in shapes),
                pltpu.SemaphoreType.DMA((4,)),
            ],
            compiler_params=pltpu.CompilerParams(vmem_limit_bytes=64 * 2**20),
        )(*results)

    placed = (
        P("section", "dp", "expert", None),
        P("section", "dp", "expert", None, None),
        P("section", "expert", None, None),
        P("section", "expert", None),
        P("section", "dp", "expert", None),
        P("section", "dp", "expert", None),
        P("section", "dp", "expert", None),
        P("section", "dp", "expert", None),
    )
    return jax.shard_map(
        step,
        mesh=mesh,
        in_specs=placed,
        out_specs=(P("section", "dp", "expert", None), P("section", "expert", "dp")),
        check_vma=False,
    )
```
